32 devices in a mesh: segment: 2 (over core), seq: 16 (over z, y, x).
Axes of the slice: x: 2, y: 2, z: 4, core: 2. Of those that a mesh axis runs over, the one named last changes fastest.
Arguments:
- hidden: bfloat16 [2048, 2560], P('seq'), may hold values from -6 to 6
- norm_gain: float32 [2, 2560], P('segment'), may hold values from 0.1 to 1.9
- query_weight: bfloat16 [2, 2560, 2560], P('segment'), as said below
- key_weight: bfloat16 [2, 2560, 512], P('segment'), as said below
- value_weight: bfloat16 [2, 2560, 512], P('segment'), may hold values from -0.125 to 0.125
- owned_block: int32 [16], replicated, may hold values from 0 to 15, as said below
Outputs:
- layer_outputs: bfloat16 [2, 2048, 2560], P('segment', 'seq')
The draws below stay inside these ranges and needn't reach their ends.
Inputs may be any that keep to these rules, and one draw needn't show every extreme that they name: `owned_block`: each aligned run of 16 devices holds the 16 blocks of one group, each once. `query_weight`: entries scaled by the fan-in. `key_weight`: entries scaled by the fan-in.
All inputs are finite; a program needn't handle non-finite values.
Results may differ from the reference program's by a relative error of at most 0.011.
Values may be sent and summed in bfloat16 or wider, within the bound.
A program may use at most 192 MiB of HBM per device.

```python
import jax
import jax.numpy as jnp
from jax import lax

D = 2560
QH = 20
KVH = 4
HS = 128
BLK = 128
PB = 8
NC = 4
CB = 2
GROUP = 16
PROMPTS = 1
TOKENS = 2048


def shared_base(key):
    return jnp.clip(jax.random.normal(key, (2, D, QH * HS), jnp.float32), -6.0, 6.0)


def draw_query_weight(key, part):
    base = shared_base(key)
    return (base * D ** (-0.5)).astype(jnp.bfloat16)


def draw_key_weight(key, part):
    key = jax.random.fold_in(key, 5)
    fresh = jnp.clip(jax.random.normal(key, (2, D, KVH * HS), jnp.float32), -6.0, 6.0)
    mixed = fresh
    return (mixed * D ** (-0.5)).astype(jnp.bfloat16)


def draw_owned_block(key, part):
    key = jax.random.fold_in(key, 11)
    group_keys = jax.random.split(key, PROMPTS)
    orders = jax.vmap(lambda group_key: jax.random.permutation(group_key, GROUP))(group_keys)
    offsets = GROUP * jnp.arange(PROMPTS, dtype=jnp.int32)[:, None]
    return (orders.astype(jnp.int32) + offsets).reshape(-1).astype(jnp.int32)


def block_scale(stream_key, dims, cuts, low, largest):
    factor_of = 1.0
    for dim, parts in cuts:
        steps = jax.random.uniform(jax.random.fold_in(jax.random.fold_in(stream_key, 6), dim), (parts,), jnp.float32, low / len(cuts), largest / len(cuts))
        factor_of = factor_of * jnp.repeat(jnp.exp(steps), dims[dim] // parts).reshape((-1,) + (1,) * (len(dims) - 1 - dim))
    return factor_of


def scatter_about(stream_key, dims, width, bound, pieces=(), kind=jnp.bfloat16):
    entries = jax.random.normal(stream_key, dims, jnp.float32) * width
    if len(pieces) > 0:
        entries = block_scale(stream_key, dims, pieces, -0.22, 0.18) * entries
    return jnp.clip(entries, min=-bound, max=bound).astype(kind)


def setup_inputs(seed: int = 0) -> dict:
    splits = jax.random.split(jax.random.key(seed), 7)
    return {
        "hidden": scatter_about(splits[0], (TOKENS, D), 1.0, 6.0, ((0, 16),)),
        "norm_gain": jnp.clip(1.0 + 0.18 * jax.random.normal(splits[1], (2, D), jnp.float32), 0.1, 1.9),
        "query_weight": draw_query_weight(jax.random.fold_in(splits[6], 71), 0),
        "key_weight": draw_key_weight(jax.random.fold_in(splits[6], 71), 0),
        "value_weight": scatter_about(splits[4], (2, D, KVH * HS), D ** -0.5, 0.125, ((0, 2),)),
        "owned_block": draw_owned_block(jax.random.fold_in(splits[6], 71), 0),
    }


rope_base = 1000000.0
neg_fill = -1e+30
norm_eps = 1e-06

def block_meta(block_ids, row_ids, block_rows):
    local_id = block_ids % GROUP
    is_prompt = local_id < PB
    sequence = jnp.where(is_prompt, NC, (local_id - PB) // CB)
    place = jnp.where(is_prompt, local_id, PB + (local_id - PB) % CB)
    return (block_ids // GROUP, is_prompt, sequence, place * block_rows + row_ids)

def rotate(values, positions):
    half_dim = values.shape[-1] // 2
    freqs = rope_base ** (-(jnp.arange(half_dim, dtype=jnp.float32) * 2.0 / values.shape[-1]))
    angles = positions.astype(jnp.float32)[:, None] * freqs[None, :]
    cosine = jnp.cos(angles)[:, None, :]
    sine = jnp.sin(angles)[:, None, :]
    front = values[..., :half_dim]
    back = values[..., half_dim:]
    return jnp.concatenate([front * cosine - back * sine, back * cosine + front * sine], axis=-1)

def project(hidden_rows, gain, w_query, w_key, w_value, positions):
    count = hidden_rows.shape[0]
    widened = hidden_rows.astype(jnp.float32)
    meansq = lax.optimization_barrier(jnp.mean(widened * widened, axis=-1, keepdims=True))
    normed = (widened * lax.rsqrt(meansq + norm_eps) * gain).astype(jnp.bfloat16)
    query = jnp.dot(normed, w_query, preferred_element_type=jnp.float32).reshape(count, -1, HS)
    query = (rotate(query, positions) * HS ** (-0.5)).astype(jnp.bfloat16)
    key_part = jnp.dot(normed, w_key, preferred_element_type=jnp.float32).reshape(count, -1, HS)
    key_part = rotate(key_part, positions).astype(jnp.bfloat16).reshape(count, -1)
    value_part = jnp.dot(normed, w_value, preferred_element_type=jnp.float32).astype(jnp.bfloat16)
    return (query, key_part, value_part)

def layer(hidden_all, gain, w_query, w_key, w_value, owned_block):
    total_rows = hidden_all.shape[0]
    token_ids = jnp.arange(total_rows, dtype=jnp.int32)
    device_ids = token_ids // BLK
    group_of, prompt_of, seq_of, pos_of = block_meta(owned_block[device_ids], token_ids % BLK, BLK)
    query, key_all, value_all = project(hidden_all, gain, w_query, w_key, w_value, pos_of)
    query, key_all, value_all = lax.optimization_barrier((query, key_all, value_all))
    span = GROUP * BLK
    repeat_count = QH // KVH

    def one_device(device):
        q_start = (device * BLK).astype(jnp.int32)
        k_start = (device // GROUP * span).astype(jnp.int32)
        q_rows = lax.dynamic_slice_in_dim(query, q_start, BLK, 0).astype(jnp.float32)
        q_rows = q_rows.reshape(BLK, KVH, repeat_count, HS)
        k_rows = lax.dynamic_slice_in_dim(key_all, k_start, span, 0).astype(jnp.float32).reshape(span, KVH, HS)
        v_rows = lax.dynamic_slice_in_dim(value_all, k_start, span, 0).astype(jnp.float32).reshape(span, KVH, HS)
        q_grp = lax.dynamic_slice_in_dim(group_of, q_start, BLK, 0)
        q_prompt = lax.dynamic_slice_in_dim(prompt_of, q_start, BLK, 0)
        q_seq = lax.dynamic_slice_in_dim(seq_of, q_start, BLK, 0)
        q_pos = lax.dynamic_slice_in_dim(pos_of, q_start, BLK, 0)
        k_grp = lax.dynamic_slice_in_dim(group_of, k_start, span, 0)
        k_prompt = lax.dynamic_slice_in_dim(prompt_of, k_start, span, 0)
        k_seq = lax.dynamic_slice_in_dim(seq_of, k_start, span, 0)
        k_pos = lax.dynamic_slice_in_dim(pos_of, k_start, span, 0)
        allowed = (k_grp[None, :] == q_grp[:, None]) & (k_prompt[None, :] & jnp.logical_not(q_prompt[:, None]) | (k_seq[None, :] == q_seq[:, None]) & (k_pos[None, :] <= q_pos[:, None]))
        scores = jnp.einsum('ngrd,lgd->grnl', q_rows, k_rows)
        scores = jnp.where(allowed[None, None], scores, neg_fill)
        top = lax.optimization_barrier(jnp.max(scores, axis=-1, keepdims=True))
        weights = jnp.where(allowed[None, None], jnp.exp(scores - top), 0.0)
        total_w = lax.optimization_barrier(jnp.sum(weights, axis=-1))
        rounded = lax.optimization_barrier(weights.astype(jnp.bfloat16))
        mixed = jnp.einsum('grnl,lgd->grnd', rounded.astype(jnp.float32), v_rows) / total_w[..., None]
        heads_out = mixed.transpose(2, 0, 1, 3).reshape(BLK, QH * HS)
        own_rows = lax.dynamic_slice_in_dim(hidden_all, q_start, BLK, 0).astype(jnp.float32)
        return (own_rows + heads_out).astype(jnp.bfloat16)
    blocks_out = lax.map(one_device, jnp.arange(total_rows // BLK, dtype=jnp.int32))
    return blocks_out.reshape(total_rows, -1)

def reference(hidden, norm_gain, query_weight, key_weight, value_weight, owned_block):
    first_out = layer(hidden, norm_gain[0], query_weight[0], key_weight[0], value_weight[0], owned_block)
    second_out = layer(first_out, norm_gain[1], query_weight[1], key_weight[1], value_weight[1], owned_block)
    return jnp.stack([first_out, second_out])
```

```python
import functools

import jax
import jax.numpy as jnp
import numpy as np
from jax import lax
from jax.experimental import pallas as pl
from jax.experimental.pallas import tpu as pltpu
from jax.sharding import PartitionSpec as P

HS = 128
PB = 8
CB = 2
GROUP = 16
PLACES = PB + CB
PLANE = 4
PLANES = GROUP // PLANE

ROPE_BASE = 1000000.0
NEG = -1e30
EPS = 1e-06
MESH = pl.DeviceIdType.MESH
F32 = jnp.float32
BF16 = jnp.bfloat16


def rope_table(rows):
    half = HS // 2
    freqs = ROPE_BASE ** (-(np.arange(half) * 2.0 / HS))
    angles = np.arange(PLACES * rows)[:, None] * freqs[None, :]
    cosine, sine = np.cos(angles), np.sin(angles)
    table = np.stack([np.concatenate([cosine, cosine], 1), np.concatenate([-sine, sine], 1)])
    return table.reshape(2, PLACES, rows, HS).astype(np.float32)


def kernel(
    rows, kv_heads, repeat,
    owned, hidden, gain_ref, wq_hbm, wk_hbm, wv_hbm, table_ref,
    out_ref,
    x_s, normed, wq, wk, wv, q_s, keys, values, bias, top_s, total_s, acc_s,
    load_sem, send_sem, recv_sem, hand_sem,
):
    seg = lax.axis_index("segment")
    seq = lax.axis_index("seq")
    local = lax.rem(seq, GROUP)
    base = seq - local
    a, b, c = lax.rem(local, 2), lax.rem(local // 2, 2), local // PLANE
    head_cols = repeat * rows

    chunk = 4 * HS
    q_chunks = wq.shape[1] // chunk
    loads = [
        pltpu.make_async_copy(wk_hbm.at[0], wk, load_sem.at[1]),
        pltpu.make_async_copy(wv_hbm.at[0], wv, load_sem.at[2]),
    ] + [
        pltpu.make_async_copy(
            wq_hbm.at[0, :, pl.ds(i * chunk, chunk)], wq.at[:, pl.ds(i * chunk, chunk)], load_sem.at[3 + i]
        )
        for i in range(q_chunks)
    ]

    x_load = pltpu.make_async_copy(hidden, x_s, load_sem.at[0])

    @pl.when(seg == 0)
    def _():
        x_load.start()

    for load in loads:
        load.start()

    def device(a_of, b_of, c_of):
        return (seg, base + c_of * PLANE + b_of * 2 + a_of)

    x_dev, y_dev = device(1 - a, b, c), device(a, 1 - b, c)
    up_dev, down_dev = device(a, b, c + 1), device(a, b, c - 1)
    has_up, has_down = c < PLANES - 1, c > 0

    barrier = pltpu.get_barrier_semaphore()
    for target in (x_dev, y_dev, (1 - seg, seq)):
        pl.semaphore_signal(barrier, inc=1, device_id=target, device_id_type=MESH)

    @pl.when(has_up)
    def _():
        pl.semaphore_signal(barrier, inc=1, device_id=up_dev, device_id_type=MESH)

    @pl.when(has_down)
    def _():
        pl.semaphore_signal(barrier, inc=1, device_id=down_dev, device_id_type=MESH)

    pl.semaphore_wait(barrier, 3 + has_up.astype(jnp.int32) + has_down.astype(jnp.int32))

    buffers = (keys, values)

    def transfer(half, slot, target, direction, step, which):
        return pltpu.make_async_remote_copy(
            src_ref=buffers[half].at[slot],
            dst_ref=buffers[half].at[slot],
            send_sem=send_sem.at[direction, step, which],
            recv_sem=recv_sem.at[half, slot],
            device_id=target,
            device_id_type=MESH,
        )

    def arrived(half, slot):
        transfer(half, slot, x_dev, 0, 0, 0).wait_recv()

    def plane_at(step):
        if step == 0:
            return c
        low = {1: (1, 0), 2: (2, 2), 3: (3, 3)}[step]
        high = tuple(PLANES - 1 - p for p in low)
        return jnp.where(c == 0, low[0], jnp.where(c == 1, low[1], jnp.where(c == 2, high[1], high[0])))

    planes = [plane_at(step) for step in range(PLANES)]

    def slot_of(plane, a_of, b_of):
        return plane * PLANE + b_of * 2 + a_of

    def z_sends(half, step):
        plane = planes[step]
        slot = slot_of(plane, a, b)
        return (
            (has_up & (plane <= c), transfer(half, slot, up_dev, 2, step, half)),
            (has_down & (plane >= c), transfer(half, slot, down_dev, 3, step, half)),
        )

    def xy_sends(half, step):
        slot = slot_of(planes[step], a, b)
        return (transfer(half, slot, x_dev, 0, step, half), transfer(half, slot, y_dev, 1, step, half))

    def forwards(step):
        plane = planes[step]
        return (
            transfer(0, slot_of(plane, a, 1 - b), x_dev, 0, step, 2),
            transfer(1, slot_of(plane, 1 - a, b), y_dev, 1, step, 2),
        )

    def spread(half, step):
        if step > 0:
            arrived(half, slot_of(planes[step], a, b))
        for cond, copy in z_sends(half, step):
            pl.when(cond)(copy.start)
        for copy in xy_sends(half, step):
            copy.start()

    def relay(step):
        plane = planes[step]
        to_x, to_y = forwards(step)
        arrived(0, slot_of(plane, a, 1 - b))
        to_x.start()
        arrived(1, slot_of(plane, 1 - a, b))
        to_y.start()

    def gathered(step):
        plane = planes[step]
        arrived(0, slot_of(plane, 1 - a, b))
        arrived(1, slot_of(plane, a, 1 - b))
        arrived(0, slot_of(plane, 1 - a, 1 - b))
        arrived(1, slot_of(plane, 1 - a, 1 - b))

    hand = pltpu.make_async_remote_copy(
        src_ref=out_ref.at[0],
        dst_ref=x_s,
        send_sem=hand_sem.at[0],
        recv_sem=hand_sem.at[1],
        device_id=(1 - seg, seq),
        device_id_type=MESH,
    )

    mine = owned[seq]
    my_j = lax.rem(mine, GROUP)
    my_prompt = my_j < PB
    my_place = jnp.where(my_prompt, my_j, PB + lax.rem(my_j - PB + CB, CB))

    @pl.when(seg == 0)
    def _():
        x_load.wait()

    @pl.when(seg == 1)
    def _():
        hand.wait_recv()

    widened = x_s[...].astype(F32)
    meansq = jnp.mean(widened * widened, axis=-1, keepdims=True)
    normed[...] = (widened * lax.rsqrt(meansq + EPS) * gain_ref[...]).astype(BF16)

    cos_t = table_ref[0, my_place]
    sin_t = table_ref[1, my_place]

    def rotate(head):
        return head * cos_t + pltpu.roll(head, HS // 2, 1) * sin_t

    loads[0].wait()
    projected = jnp.dot(normed[...], wk[...], preferred_element_type=F32)
    for g in range(kv_heads):
        keys[local, :, g * HS : (g + 1) * HS] = rotate(projected[:, g * HS : (g + 1) * HS]).astype(BF16)
    spread(0, 0)
    loads[1].wait()
    values[local] = jnp.dot(normed[...], wv[...], preferred_element_type=F32).astype(BF16)
    spread(1, 0)

    def query_chunk(i):
        loads[2 + i].wait()
        projected = jnp.dot(normed[...], wq[:, i * chunk : (i + 1) * chunk], preferred_element_type=F32)
        for k in range(chunk // HS):
            q_s[i * (chunk // HS) + k] = (rotate(projected[:, k * HS : (k + 1) * HS]) * HS ** (-0.5)).astype(BF16)

    def attend(step):
        plane = planes[step]
        row = lax.broadcasted_iota(jnp.int32, (rows, rows), 0)
        col = lax.broadcasted_iota(jnp.int32, (rows, rows), 1)
        triangle = jnp.where(col <= row, 0.0, NEG).astype(F32)
        for i in range(PLANE):
            j = lax.rem(owned[base + plane * PLANE + i], GROUP)
            prompt = j < PB
            same = prompt == my_prompt
            pair = (j // CB) == (my_j // CB)
            full = jnp.where(prompt, (my_prompt == False) | (j < my_j), same & pair & (j < my_j))
            level = jnp.where(full, 0.0, NEG).astype(F32)
            bias[:, i * rows : (i + 1) * rows] = jnp.where(j == my_j, triangle, level)

        def one(g, carry):
            span = PLANE * rows
            cols = pl.ds(pl.multiple_of(g * HS, HS), HS)
            first = pl.multiple_of(plane * PLANE, PLANE)
            k_rows = keys[pl.ds(first, PLANE), :, cols].reshape(span, HS)
            v_rows = values[pl.ds(first, PLANE), :, cols].reshape(span, HS)
            query = q_s[pl.ds(g * repeat, repeat)].reshape(head_cols, HS)
            scores = lax.dot_general(query, k_rows, (((1,), (1,)), ((), ())), preferred_element_type=F32)
            scores = (scores.reshape(repeat, rows, span) + bias[...][None]).reshape(head_cols, span)
            best = jnp.max(scores, axis=-1, keepdims=True)
            if step == 0:
                top_new = jnp.broadcast_to(best, (head_cols, HS))
            else:
                top_old = top_s[g]
                top_new = jnp.maximum(top_old, best)
            weights = [jnp.exp(scores[:, i * HS : (i + 1) * HS] - top_new) for i in range(span // HS)]
            part = functools.reduce(jnp.add, weights)
            rounded = jnp.concatenate([w.astype(BF16) for w in weights], axis=1)
            update = jnp.dot(rounded, v_rows, preferred_element_type=F32)
            if step == 0:
                total_s[g] = part
                acc_s[g] = update
            else:
                rescale = jnp.exp(top_old - top_new)
                total_s[g] = total_s[g] * rescale + part
                acc_s[g] = acc_s[g] * rescale + update
            top_s[g] = top_new
            return carry

        lax.fori_loop(0, kv_heads, one, 0)

    half_way = (q_chunks + 1) // 2
    for i in range(half_way):
        query_chunk(i)
    relay(0)
    spread(0, 1)
    spread(1, 1)
    for i in range(half_way, q_chunks):
        query_chunk(i)
    for step in range(PLANES):
        gathered(step)
        attend(step)
        if step + 1 < PLANES:
            relay(step + 1)
            if step + 2 < PLANES:
                spread(0, step + 2)
                spread(1, step + 2)

    for g in range(kv_heads):
        total = jnp.sum(total_s[g], axis=-1, keepdims=True)
        mixed = acc_s[g] / total
        for r in range(repeat):
            lanes = slice((g * repeat + r) * HS, (g * repeat + r + 1) * HS)
            out_ref[0, :, lanes] = (
                x_s[:, lanes].astype(F32) + mixed[r * rows : (r + 1) * rows]
            ).astype(BF16)

    @pl.when(seg == 0)
    def _():
        hand.start()

    for step in range(PLANES):
        for half in range(2):
            for cond, copy in z_sends(half, step):
                pl.when(cond)(copy.wait_send)
            for copy in xy_sends(half, step):
                copy.wait_send()
        for copy in forwards(step):
            copy.wait_send()

    @pl.when(seg == 0)
    def _():
        hand.wait_send()


def section(hidden, norm_gain, query_weight, key_weight, value_weight, owned_block):
    rows, width = hidden.shape
    q_cols, kv_cols = query_weight.shape[2], key_weight.shape[2]
    heads, kv_heads = q_cols // HS, kv_cols // HS
    repeat = heads // kv_heads
    any_spec = pl.BlockSpec(memory_space=pl.ANY)
    vmem_spec = pl.BlockSpec(memory_space=pltpu.VMEM)
    state = pltpu.VMEM((kv_heads, repeat * rows, HS), F32)
    return pl.pallas_call(
        functools.partial(kernel, rows, kv_heads, repeat),
        out_shape=jax.ShapeDtypeStruct((1, rows, q_cols), BF16),
        in_specs=[
            pl.BlockSpec(memory_space=pltpu.SMEM),
            any_spec,
            vmem_spec,
            any_spec,
            any_spec,
            any_spec,
            vmem_spec,
        ],
        out_specs=vmem_spec,
        scratch_shapes=[
            pltpu.VMEM((rows, width), BF16),
            pltpu.VMEM((rows, width), BF16),
            pltpu.VMEM((width, q_cols), BF16),
            pltpu.VMEM((width, kv_cols), BF16),
            pltpu.VMEM((width, kv_cols), BF16),
            pltpu.VMEM((heads, rows, HS), BF16),
            pltpu.VMEM((GROUP, rows, kv_cols), BF16),
            pltpu.VMEM((GROUP, rows, kv_cols), BF16),
            pltpu.VMEM((rows, PLANE * rows), F32),
            state,
            state,
            state,
            pltpu.SemaphoreType.DMA((3 + q_cols // (4 * HS),)),
            pltpu.SemaphoreType.DMA((4, PLANES, 3)),
            pltpu.SemaphoreType.DMA((2, GROUP)),
            pltpu.SemaphoreType.DMA((2,)),
        ],
        compiler_params=pltpu.CompilerParams(
            collective_id=0, has_side_effects=True, vmem_limit_bytes=56 * 1024 * 1024
        ),
        cost_estimate=pl.CostEstimate(
            flops=2 * rows * width * (q_cols + 2 * kv_cols) + 4 * rows * rows * GROUP * q_cols,
            bytes_accessed=2 * width * (q_cols + 2 * kv_cols),
            transcendentals=rows * rows * GROUP * heads,
        ),
    )(owned_block, hidden, norm_gain, query_weight, key_weight, value_weight, jnp.asarray(rope_table(rows)))


def solution(mesh):
    return jax.shard_map(
        section,
        mesh=mesh,
        in_specs=(
            P("seq", None),
            P("segment", None),
            P("segment", None, None),
            P("segment", None, None),
            P("segment", None, None),
            P(),
        ),
        out_specs=P("segment", "seq", None),
        check_vma=False,
    )
```

```python
import functools

import jax
import jax.numpy as jnp
import numpy as np
from jax import lax
from jax.experimental import pallas as pl
from jax.experimental.pallas import tpu as pltpu
from jax.sharding import PartitionSpec as P

HS = 128
PB = 8
CB = 2
GROUP = 16
PLACES = PB + CB
PLANE = 4
PLANES = GROUP // PLANE

ROPE_BASE = 1000000.0
NEG = -1e30
SCALE = HS ** (-0.5) * float(np.log2(np.e))
EPS = 1e-06
UNROLL = 4
REACH = 2
MESH = pl.DeviceIdType.MESH
F32 = jnp.float32
BF16 = jnp.bfloat16


def rope_table(rows):
    half = HS // 2
    freqs = ROPE_BASE ** (-(np.arange(half) * 2.0 / HS))
    angles = np.arange(PLACES * rows)[:, None] * freqs[None, :]
    cosine, sine = np.cos(angles), np.sin(angles)
    table = np.stack([np.concatenate([cosine, cosine], 1), np.concatenate([-sine, sine], 1)])
    return table.reshape(2, PLACES, rows, HS).astype(np.float32)


def kernel(
    rows, kv_heads, repeat,
    owned, hidden, gain_ref, wq_hbm, wk_hbm, wv_hbm, table_ref,
    out_ref,
    x_s, normed, wq, wk, wv, q_s, keys, values, bias, top_s, acc_s,
    load_sem, send_sem, recv_sem, hand_sem,
):
    seg = lax.axis_index("segment")
    seq = lax.axis_index("seq")
    local = lax.rem(seq, GROUP)
    base = seq - local
    a, b, c = lax.rem(local, 2), lax.rem(local // 2, 2), local // PLANE
    head_cols = repeat * rows

    chunk = 4 * HS
    q_chunks = wq.shape[1] // chunk
    loads = [
        pltpu.make_async_copy(wk_hbm.at[0], wk, load_sem.at[1]),
        pltpu.make_async_copy(wv_hbm.at[0], wv, load_sem.at[2]),
    ] + [
        pltpu.make_async_copy(
            wq_hbm.at[0, :, pl.ds(i * chunk, chunk)], wq.at[:, pl.ds(i * chunk, chunk)], load_sem.at[3 + i]
        )
        for i in range(q_chunks)
    ]

    x_load = pltpu.make_async_copy(hidden, x_s, load_sem.at[0])

    @pl.when(seg == 0)
    def _():
        x_load.start()

    for load in loads:
        load.start()

    def device(a_of, b_of, c_of):
        return (seg, base + c_of * PLANE + b_of * 2 + a_of)

    x_dev, y_dev = device(1 - a, b, c), device(a, 1 - b, c)
    up_dev, down_dev = device(a, b, c + 1), device(a, b, c - 1)
    has_up, has_down = c < PLANES - 1, c > 0

    barrier = pltpu.get_barrier_semaphore()
    for target in (x_dev, y_dev, (1 - seg, seq)):
        pl.semaphore_signal(barrier, inc=1, device_id=target, device_id_type=MESH)

    @pl.when(has_up)
    def _():
        pl.semaphore_signal(barrier, inc=1, device_id=up_dev, device_id_type=MESH)

    @pl.when(has_down)
    def _():
        pl.semaphore_signal(barrier, inc=1, device_id=down_dev, device_id_type=MESH)

    pl.semaphore_wait(barrier, 3 + has_up.astype(jnp.int32) + has_down.astype(jnp.int32))

    buffers = (keys, values)

    def transfer(half, slot, target, direction, step, which):
        return pltpu.make_async_remote_copy(
            src_ref=buffers[half].at[slot],
            dst_ref=buffers[half].at[slot],
            send_sem=send_sem.at[direction, step, which],
            recv_sem=recv_sem.at[half, slot],
            device_id=target,
            device_id_type=MESH,
        )

    def arrived(half, slot):
        transfer(half, slot, x_dev, 0, 0, 0).wait_recv()

    def plane_at(step):
        if step == 0:
            return c
        low = {1: (1, 0), 2: (2, 2), 3: (3, 3)}[step]
        high = tuple(PLANES - 1 - p for p in low)
        return jnp.where(c == 0, low[0], jnp.where(c == 1, low[1], jnp.where(c == 2, high[1], high[0])))

    planes = [plane_at(step) for step in range(PLANES)]

    def slot_of(plane, a_of, b_of):
        return plane * PLANE + b_of * 2 + a_of

    def z_sends(half, step):
        plane = planes[step]
        slot = slot_of(plane, a, b)
        return (
            (has_up & (plane <= c), transfer(half, slot, up_dev, 2, step, half)),
            (has_down & (plane >= c), transfer(half, slot, down_dev, 3, step, half)),
        )

    def xy_sends(half, step):
        slot = slot_of(planes[step], a, b)
        return (transfer(half, slot, x_dev, 0, step, half), transfer(half, slot, y_dev, 1, step, half))

    def forwards(step):
        plane = planes[step]
        return (
            transfer(0, slot_of(plane, a, 1 - b), x_dev, 0, step, 2),
            transfer(1, slot_of(plane, 1 - a, b), y_dev, 1, step, 2),
        )

    def near(plane):
        return (plane - c <= REACH) & (c - plane <= REACH)

    def diagonals(step):
        plane = planes[step]
        slot = slot_of(plane, 1 - a, 1 - b)
        go_up = has_up & (plane <= c) & (c + 1 - plane <= REACH)
        go_down = has_down & (plane >= c) & (plane - c + 1 <= REACH)
        return tuple(
            (cond, transfer(half, slot, target, direction, step, 2 + half))
            for half in range(2)
            for cond, target, direction in ((go_up, up_dev, 2), (go_down, down_dev, 3))
        )

    def spread(half, step):
        if step > 0:
            arrived(half, slot_of(planes[step], a, b))
        for cond, copy in z_sends(half, step):
            pl.when(cond)(copy.start)
        for copy in xy_sends(half, step):
            copy.start()

    def relay(step):
        plane = planes[step]
        to_x, to_y = forwards(step)
        arrived(0, slot_of(plane, a, 1 - b))
        if step == 0:
            to_x.start()
        else:
            pl.when(jnp.logical_not(near(plane)))(to_x.start)
        arrived(1, slot_of(plane, 1 - a, b))
        if step == 0:
            to_y.start()
        else:
            pl.when(jnp.logical_not(near(plane)))(to_y.start)

    def gathered(step):
        plane = planes[step]
        arrived(0, slot_of(plane, 1 - a, b))
        arrived(1, slot_of(plane, a, 1 - b))
        arrived(0, slot_of(plane, 1 - a, 1 - b))
        arrived(1, slot_of(plane, 1 - a, 1 - b))
        if step + 1 < PLANES:
            for cond, copy in diagonals(step):
                pl.when(cond)(copy.start)

    hand = pltpu.make_async_remote_copy(
        src_ref=out_ref.at[0],
        dst_ref=x_s,
        send_sem=hand_sem.at[0],
        recv_sem=hand_sem.at[1],
        device_id=(1 - seg, seq),
        device_id_type=MESH,
    )

    mine = owned[seq]
    my_j = lax.rem(mine, GROUP)
    my_prompt = my_j < PB
    my_place = jnp.where(my_prompt, my_j, PB + lax.rem(my_j - PB + CB, CB))

    @pl.when(seg == 0)
    def _():
        x_load.wait()

    @pl.when(seg == 1)
    def _():
        hand.wait_recv()

    widened = x_s[...].astype(F32)
    meansq = jnp.mean(widened * widened, axis=-1, keepdims=True)
    normed[...] = (widened * lax.rsqrt(meansq + EPS) * gain_ref[...]).astype(BF16)

    cos_t = table_ref[0, my_place]
    sin_t = table_ref[1, my_place]

    def rotate(head):
        return head * cos_t + pltpu.roll(head, HS // 2, 1) * sin_t

    loads[0].wait()
    projected = jnp.dot(normed[...], wk[...], preferred_element_type=F32)
    for g in range(kv_heads):
        keys[local, :, g * HS : (g + 1) * HS] = rotate(projected[:, g * HS : (g + 1) * HS]).astype(BF16)
    spread(0, 0)
    loads[1].wait()
    values[local] = jnp.dot(normed[...], wv[...], preferred_element_type=F32).astype(BF16)
    spread(1, 0)

    eye = lax.broadcasted_iota(jnp.int32, (rows, rows), 0) == lax.broadcasted_iota(jnp.int32, (rows, rows), 1)
    for h in range(kv_heads * repeat):
        q_s[h, :, HS:] = eye.astype(F32).astype(BF16)

    def query_chunk(i):
        loads[2 + i].wait()
        projected = jnp.dot(normed[...], wq[:, i * chunk : (i + 1) * chunk], preferred_element_type=F32)
        for k in range(chunk // HS):
            q_s[i * (chunk // HS) + k, :, :HS] = (rotate(projected[:, k * HS : (k + 1) * HS]) * SCALE).astype(BF16)

    def attend(step):
        plane = planes[step]
        row = lax.broadcasted_iota(jnp.int32, (rows, rows), 0)
        col = lax.broadcasted_iota(jnp.int32, (rows, rows), 1)
        triangle = jnp.where(row <= col, 0.0, NEG).astype(F32)
        for i in range(PLANE):
            j = lax.rem(owned[base + plane * PLANE + i], GROUP)
            prompt = j < PB
            same = prompt == my_prompt
            pair = (j // CB) == (my_j // CB)
            full = jnp.where(prompt, (my_prompt == False) | (j < my_j), same & pair & (j < my_j))
            level = jnp.where(full, 0.0, NEG).astype(F32)
            bias[i * rows : (i + 1) * rows] = jnp.where(j == my_j, triangle, level).astype(BF16)

        def one(g, carry):
            span = PLANE * rows
            cols = pl.ds(pl.multiple_of(g * HS, HS), HS)
            first = pl.multiple_of(plane * PLANE, PLANE)
            k_rows = keys[pl.ds(first, PLANE), :, cols].reshape(span, HS)
            v_rows = values[pl.ds(first, PLANE), :, cols].reshape(span, HS)
            query = q_s[pl.ds(g * repeat, repeat)].reshape(head_cols, HS + rows)
            k_wide = jnp.concatenate([k_rows, bias[...]], axis=1)
            v_wide = jnp.concatenate([v_rows, jnp.ones((span, HS), BF16)], axis=1)
            scores = lax.dot_general(query, k_wide, (((1,), (1,)), ((), ())), preferred_element_type=F32)
            best = jnp.max(scores, axis=-1, keepdims=True)
            if step == 0:
                top_new = jnp.broadcast_to(best, (head_cols, HS))
            else:
                top_old = top_s[g]
                top_new = jnp.maximum(top_old, best)
            weights = [jnp.exp2(scores[:, i * HS : (i + 1) * HS] - top_new) for i in range(span // HS)]
            rounded = jnp.concatenate([w.astype(BF16) for w in weights], axis=1)
            update = jnp.dot(rounded, v_wide, preferred_element_type=F32)
            if step == 0:
                acc_s[g] = update
            else:
                rescale = jnp.exp2(top_old - top_new)
                acc_s[g] = acc_s[g] * jnp.concatenate([rescale, rescale], axis=1) + update
            top_s[g] = top_new
            return carry

        lax.fori_loop(0, kv_heads, one, 0, unroll=UNROLL)

    half_way = (q_chunks + 1) // 2
    for i in range(half_way):
        query_chunk(i)
    relay(0)
    spread(0, 1)
    spread(1, 1)
    for i in range(half_way, q_chunks):
        query_chunk(i)
    gathered(0)
    spread(0, 2)
    spread(1, 2)
    spread(0, 3)
    spread(1, 3)
    attend(0)
    relay(1)
    gathered(1)
    attend(1)
    relay(2)
    gathered(2)
    relay(3)
    attend(2)
    gathered(3)
    attend(3)

    for g in range(kv_heads):
        mixed = acc_s[g, :, :HS] / acc_s[g, :, HS:]
        for r in range(repeat):
            lanes = slice((g * repeat + r) * HS, (g * repeat + r + 1) * HS)
            out_ref[0, :, lanes] = (
                x_s[:, lanes].astype(F32) + mixed[r * rows : (r + 1) * rows]
            ).astype(BF16)

    @pl.when(seg == 0)
    def _():
        hand.start()

    for step in range(PLANES):
        for half in range(2):
            for cond, copy in z_sends(half, step):
                pl.when(cond)(copy.wait_send)
            for copy in xy_sends(half, step):
                copy.wait_send()
        if step + 1 < PLANES:
            for cond, copy in diagonals(step):
                pl.when(cond)(copy.wait_send)
        for copy in forwards(step):
            if step == 0:
                copy.wait_send()
            else:
                pl.when(jnp.logical_not(near(planes[step])))(copy.wait_send)

    @pl.when(seg == 0)
    def _():
        hand.wait_send()


def section(hidden, norm_gain, query_weight, key_weight, value_weight, owned_block):
    rows, width = hidden.shape
    q_cols, kv_cols = query_weight.shape[2], key_weight.shape[2]
    heads, kv_heads = q_cols // HS, kv_cols // HS
    repeat = heads // kv_heads
    any_spec = pl.BlockSpec(memory_space=pl.ANY)
    vmem_spec = pl.BlockSpec(memory_space=pltpu.VMEM)
    return pl.pallas_call(
        functools.partial(kernel, rows, kv_heads, repeat),
        out_shape=jax.ShapeDtypeStruct((1, rows, q_cols), BF16),
        in_specs=[
            pl.BlockSpec(memory_space=pltpu.SMEM),
            any_spec,
            vmem_spec,
            any_spec,
            any_spec,
            any_spec,
            vmem_spec,
        ],
        out_specs=vmem_spec,
        scratch_shapes=[
            pltpu.VMEM((rows, width), BF16),
            pltpu.VMEM((rows, width), BF16),
            pltpu.VMEM((width, q_cols), BF16),
            pltpu.VMEM((width, kv_cols), BF16),
            pltpu.VMEM((width, kv_cols), BF16),
            pltpu.VMEM((heads, rows, HS + rows), BF16),
            pltpu.VMEM((GROUP, rows, kv_cols), BF16),
            pltpu.VMEM((GROUP, rows, kv_cols), BF16),
            pltpu.VMEM((PLANE * rows, rows), BF16),
            pltpu.VMEM((kv_heads, repeat * rows, HS), F32),
            pltpu.VMEM((kv_heads, repeat * rows, 2 * HS), F32),
            pltpu.SemaphoreType.DMA((3 + q_cols // (4 * HS),)),
            pltpu.SemaphoreType.DMA((4, PLANES, 4)),
            pltpu.SemaphoreType.DMA((2, GROUP)),
            pltpu.SemaphoreType.DMA((2,)),
        ],
        compiler_params=pltpu.CompilerParams(
            collective_id=0, has_side_effects=True, vmem_limit_bytes=56 * 1024 * 1024
        ),
        cost_estimate=pl.CostEstimate(
            flops=2 * rows * width * (q_cols + 2 * kv_cols) + 4 * rows * rows * GROUP * q_cols,
            bytes_accessed=2 * width * (q_cols + 2 * kv_cols),
            transcendentals=rows * rows * GROUP * heads,
        ),
    )(owned_block, hidden, norm_gain, query_weight, key_weight, value_weight, jnp.asarray(rope_table(rows)))


def solution(mesh):
    return jax.shard_map(
        section,
        mesh=mesh,
        in_specs=(
            P("seq", None),
            P("segment", None),
            P("segment", None, None),
            P("segment", None, None),
            P("segment", None, None),
            P(),
        ),
        out_specs=P("segment", "seq", None),
        check_vma=False,
    )
```

```python
import functools

import jax
import jax.numpy as jnp
import numpy as np
from jax import lax
from jax.experimental import pallas as pl
from jax.experimental.pallas import tpu as pltpu
from jax.sharding import PartitionSpec as P

HS = 128
PB = 8
CB = 2
GROUP = 16
PLACES = PB + CB
PLANE = 4
PLANES = GROUP // PLANE

ROPE_BASE = 1000000.0
NEG = -1e30
SCALE = HS ** (-0.5) * float(np.log2(np.e))
EPS = 1e-06
UNROLL = 4
REACH = 2
MESH = pl.DeviceIdType.MESH
F32 = jnp.float32
BF16 = jnp.bfloat16


def rope_table(rows):
    half = HS // 2
    freqs = ROPE_BASE ** (-(np.arange(half) * 2.0 / HS))
    angles = np.arange(PLACES * rows)[:, None] * freqs[None, :]
    cosine, sine = np.cos(angles), np.sin(angles)
    table = np.stack([np.concatenate([cosine, cosine], 1), np.concatenate([-sine, sine], 1)])
    return table.reshape(2, PLACES, rows, HS).astype(np.float32)


def kernel(
    rows, kv_heads, repeat,
    owned, hidden, gain_ref, wq_hbm, wk_hbm, wv_hbm, table_ref,
    out_ref,
    x_s, normed, wq, wk, wv, q_s, keys, values, bias, top_s, acc_s,
    load_sem, send_sem, recv_sem, hand_sem,
):
    seg = lax.axis_index("segment")
    seq = lax.axis_index("seq")
    local = lax.rem(seq, GROUP)
    base = seq - local
    a, b, c = lax.rem(local, 2), lax.rem(local // 2, 2), local // PLANE
    head_cols = repeat * rows

    chunk = 4 * HS
    q_chunks = wq.shape[1] // chunk
    loads = [
        pltpu.make_async_copy(wk_hbm.at[0], wk, load_sem.at[1]),
        pltpu.make_async_copy(wv_hbm.at[0], wv, load_sem.at[2]),
    ] + [
        pltpu.make_async_copy(
            wq_hbm.at[0, :, pl.ds(i * chunk, chunk)], wq.at[:, pl.ds(i * chunk, chunk)], load_sem.at[3 + i]
        )
        for i in range(q_chunks)
    ]

    x_load = pltpu.make_async_copy(hidden, x_s, load_sem.at[0])

    @pl.when(seg == 0)
    def _():
        x_load.start()

    for load in loads[:2]:
        load.start()

    def device(a_of, b_of, c_of):
        return (seg, base + c_of * PLANE + b_of * 2 + a_of)

    x_dev, y_dev = device(1 - a, b, c), device(a, 1 - b, c)
    up_dev, down_dev = device(a, b, c + 1), device(a, b, c - 1)
    has_up, has_down = c < PLANES - 1, c > 0

    barrier = pltpu.get_barrier_semaphore()
    for target in (x_dev, y_dev, (1 - seg, seq)):
        pl.semaphore_signal(barrier, inc=1, device_id=target, device_id_type=MESH)

    @pl.when(has_up)
    def _():
        pl.semaphore_signal(barrier, inc=1, device_id=up_dev, device_id_type=MESH)

    @pl.when(has_down)
    def _():
        pl.semaphore_signal(barrier, inc=1, device_id=down_dev, device_id_type=MESH)

    pl.semaphore_wait(barrier, 3 + has_up.astype(jnp.int32) + has_down.astype(jnp.int32))

    buffers = (keys, values)

    def transfer(half, slot, target, direction, step, which):
        return pltpu.make_async_remote_copy(
            src_ref=buffers[half].at[slot],
            dst_ref=buffers[half].at[slot],
            send_sem=send_sem.at[direction, step, which],
            recv_sem=recv_sem.at[half, slot],
            device_id=target,
            device_id_type=MESH,
        )

    def arrived(half, slot):
        transfer(half, slot, x_dev, 0, 0, 0).wait_recv()

    def plane_at(step):
        if step == 0:
            return c
        low = {1: (1, 0), 2: (2, 2), 3: (3, 3)}[step]
        high = tuple(PLANES - 1 - p for p in low)
        return jnp.where(c == 0, low[0], jnp.where(c == 1, low[1], jnp.where(c == 2, high[1], high[0])))

    planes = [plane_at(step) for step in range(PLANES)]

    def slot_of(plane, a_of, b_of):
        return plane * PLANE + b_of * 2 + a_of

    def z_sends(half, step):
        plane = planes[step]
        slot = slot_of(plane, a, b)
        return (
            (has_up & (plane <= c), transfer(half, slot, up_dev, 2, step, half)),
            (has_down & (plane >= c), transfer(half, slot, down_dev, 3, step, half)),
        )

    def xy_sends(half, step):
        slot = slot_of(planes[step], a, b)
        return (transfer(half, slot, x_dev, 0, step, half), transfer(half, slot, y_dev, 1, step, half))

    def forwards(step):
        plane = planes[step]
        return (
            transfer(0, slot_of(plane, a, 1 - b), x_dev, 0, step, 2),
            transfer(1, slot_of(plane, 1 - a, b), y_dev, 1, step, 2),
        )

    def near(plane):
        return (plane - c <= REACH) & (c - plane <= REACH)

    def diagonals(step):
        plane = planes[step]
        slot = slot_of(plane, 1 - a, 1 - b)
        go_up = has_up & (plane <= c) & (c + 1 - plane <= REACH)
        go_down = has_down & (plane >= c) & (plane - c + 1 <= REACH)
        return tuple(
            (cond, transfer(half, slot, target, direction, step, 2 + half))
            for half in range(2)
            for cond, target, direction in ((go_up, up_dev, 2), (go_down, down_dev, 3))
        )

    def spread(half, step):
        if step > 0:
            arrived(half, slot_of(planes[step], a, b))
        for cond, copy in z_sends(half, step):
            pl.when(cond)(copy.start)
        for copy in xy_sends(half, step):
            copy.start()

    def relay(step):
        plane = planes[step]
        to_x, to_y = forwards(step)
        arrived(0, slot_of(plane, a, 1 - b))
        if step == 0:
            to_x.start()
        else:
            pl.when(jnp.logical_not(near(plane)))(to_x.start)
        arrived(1, slot_of(plane, 1 - a, b))
        if step == 0:
            to_y.start()
        else:
            pl.when(jnp.logical_not(near(plane)))(to_y.start)

    def gathered(step):
        plane = planes[step]
        arrived(0, slot_of(plane, 1 - a, b))
        arrived(1, slot_of(plane, a, 1 - b))
        arrived(0, slot_of(plane, 1 - a, 1 - b))
        arrived(1, slot_of(plane, 1 - a, 1 - b))
        if step + 1 < PLANES:
            for cond, copy in diagonals(step):
                pl.when(cond)(copy.start)

    hand = pltpu.make_async_remote_copy(
        src_ref=out_ref.at[0],
        dst_ref=x_s,
        send_sem=hand_sem.at[0],
        recv_sem=hand_sem.at[1],
        device_id=(1 - seg, seq),
        device_id_type=MESH,
    )

    mine = owned[seq]
    my_j = lax.rem(mine, GROUP)
    my_prompt = my_j < PB
    my_place = jnp.where(my_prompt, my_j, PB + lax.rem(my_j - PB + CB, CB))

    @pl.when(seg == 0)
    def _():
        x_load.wait()

    @pl.when(seg == 1)
    def _():
        hand.wait_recv()

    widened = x_s[...].astype(F32)
    meansq = jnp.mean(widened * widened, axis=-1, keepdims=True)
    normed[...] = (widened * lax.rsqrt(meansq + EPS) * gain_ref[...]).astype(BF16)

    cos_t = table_ref[0, my_place]
    sin_t = table_ref[1, my_place]

    def rotate(head):
        return head * cos_t + pltpu.roll(head, HS // 2, 1) * sin_t

    loads[0].wait()
    for load in loads[2:]:
        load.start()
    projected = jnp.dot(normed[...], wk[...], preferred_element_type=F32)
    for g in range(kv_heads):
        keys[local, :, g * HS : (g + 1) * HS] = rotate(projected[:, g * HS : (g + 1) * HS]).astype(BF16)
    spread(0, 0)
    loads[1].wait()
    values[local] = jnp.dot(normed[...], wv[...], preferred_element_type=F32).astype(BF16)
    spread(1, 0)

    eye = lax.broadcasted_iota(jnp.int32, (rows, rows), 0) == lax.broadcasted_iota(jnp.int32, (rows, rows), 1)
    for h in range(kv_heads * repeat):
        q_s[h, :, HS:] = eye.astype(F32).astype(BF16)

    def query_chunk(i):
        loads[2 + i].wait()
        projected = jnp.dot(normed[...], wq[:, i * chunk : (i + 1) * chunk], preferred_element_type=F32)
        for k in range(chunk // HS):
            q_s[i * (chunk // HS) + k, :, :HS] = (rotate(projected[:, k * HS : (k + 1) * HS]) * SCALE).astype(BF16)

    def attend(step, first, count):
        row = lax.broadcasted_iota(jnp.int32, (rows, rows), 0)
        col = lax.broadcasted_iota(jnp.int32, (rows, rows), 1)
        triangle = jnp.where(row <= col, 0.0, NEG).astype(F32)
        for i in range(count):
            j = lax.rem(owned[base + first + i], GROUP)
            prompt = j < PB
            same = prompt == my_prompt
            pair = (j // CB) == (my_j // CB)
            full = jnp.where(prompt, (my_prompt == False) | (j < my_j), same & pair & (j < my_j))
            level = jnp.where(full, 0.0, NEG).astype(F32)
            bias[i * rows : (i + 1) * rows] = jnp.where(j == my_j, triangle, level).astype(BF16)

        def one(g, carry):
            span = count * rows
            cols = pl.ds(pl.multiple_of(g * HS, HS), HS)
            k_rows = keys[pl.ds(first, count), :, cols].reshape(span, HS)
            v_rows = values[pl.ds(first, count), :, cols].reshape(span, HS)
            query = q_s[pl.ds(g * repeat, repeat)].reshape(head_cols, HS + rows)
            k_wide = jnp.concatenate([k_rows, bias[:span]], axis=1)
            v_wide = jnp.concatenate([v_rows, jnp.ones((span, HS), BF16)], axis=1)
            scores = lax.dot_general(query, k_wide, (((1,), (1,)), ((), ())), preferred_element_type=F32)
            best = jnp.max(scores, axis=-1, keepdims=True)
            if step == 0:
                top_new = jnp.broadcast_to(best, (head_cols, HS))
            else:
                top_old = top_s[g]
                top_new = jnp.maximum(top_old, best)
            weights = [jnp.exp2(scores[:, i * HS : (i + 1) * HS] - top_new) for i in range(span // HS)]
            rounded = jnp.concatenate([w.astype(BF16) for w in weights], axis=1)
            update = jnp.dot(rounded, v_wide, preferred_element_type=F32)
            if step == 0:
                acc_s[g] = update
            else:
                rescale = jnp.exp2(top_old - top_new)
                acc_s[g] = acc_s[g] * jnp.concatenate([rescale, rescale], axis=1) + update
            top_s[g] = top_new
            return carry

        lax.fori_loop(0, kv_heads, one, 0, unroll=UNROLL)

    half_way = (q_chunks + 1) // 2
    for i in range(half_way):
        query_chunk(i)
    relay(0)
    spread(0, 1)
    spread(1, 1)
    for i in range(half_way, q_chunks):
        query_chunk(i)
    gathered(0)
    spread(0, 2)
    spread(1, 2)
    spread(0, 3)
    spread(1, 3)
    attend(0, planes[0] * PLANE, PLANE)
    relay(1)
    gathered(1)
    attend(1, planes[1] * PLANE, PLANE)
    relay(2)
    gathered(2)
    relay(3)
    attend(2, planes[2] * PLANE, PLANE)
    last = planes[3] * PLANE
    arrived(0, slot_of(planes[3], 1 - a, b))
    attend(3, last + 2 * b, 2)
    arrived(1, slot_of(planes[3], a, 1 - b))
    arrived(0, slot_of(planes[3], 1 - a, 1 - b))
    arrived(1, slot_of(planes[3], 1 - a, 1 - b))
    attend(3, last + 2 * (1 - b), 2)

    for g in range(kv_heads):
        mixed = acc_s[g, :, :HS] / acc_s[g, :, HS:]
        for r in range(repeat):
            lanes = slice((g * repeat + r) * HS, (g * repeat + r + 1) * HS)
            out_ref[0, :, lanes] = (
                x_s[:, lanes].astype(F32) + mixed[r * rows : (r + 1) * rows]
            ).astype(BF16)

    @pl.when(seg == 0)
    def _():
        hand.start()

    for step in range(PLANES):
        for half in range(2):
            for cond, copy in z_sends(half, step):
                pl.when(cond)(copy.wait_send)
            for copy in xy_sends(half, step):
                copy.wait_send()
        if step + 1 < PLANES:
            for cond, copy in diagonals(step):
                pl.when(cond)(copy.wait_send)
        for copy in forwards(step):
            if step == 0:
                copy.wait_send()
            else:
                pl.when(jnp.logical_not(near(planes[step])))(copy.wait_send)

    @pl.when(seg == 0)
    def _():
        hand.wait_send()


def section(hidden, norm_gain, query_weight, key_weight, value_weight, owned_block):
    rows, width = hidden.shape
    q_cols, kv_cols = query_weight.shape[2], key_weight.shape[2]
    heads, kv_heads = q_cols // HS, kv_cols // HS
    repeat = heads // kv_heads
    any_spec = pl.BlockSpec(memory_space=pl.ANY)
    vmem_spec = pl.BlockSpec(memory_space=pltpu.VMEM)
    return pl.pallas_call(
        functools.partial(kernel, rows, kv_heads, repeat),
        out_shape=jax.ShapeDtypeStruct((1, rows, q_cols), BF16),
        in_specs=[
            pl.BlockSpec(memory_space=pltpu.SMEM),
            any_spec,
            vmem_spec,
            any_spec,
            any_spec,
            any_spec,
            vmem_spec,
        ],
        out_specs=vmem_spec,
        scratch_shapes=[
            pltpu.VMEM((rows, width), BF16),
            pltpu.VMEM((rows, width), BF16),
            pltpu.VMEM((width, q_cols), BF16),
            pltpu.VMEM((width, kv_cols), BF16),
            pltpu.VMEM((width, kv_cols), BF16),
            pltpu.VMEM((heads, rows, HS + rows), BF16),
            pltpu.VMEM((GROUP, rows, kv_cols), BF16),
            pltpu.VMEM((GROUP, rows, kv_cols), BF16),
            pltpu.VMEM((PLANE * rows, rows), BF16),
            pltpu.VMEM((kv_heads, repeat * rows, HS), F32),
            pltpu.VMEM((kv_heads, repeat * rows, 2 * HS), F32),
            pltpu.SemaphoreType.DMA((3 + q_cols // (4 * HS),)),
            pltpu.SemaphoreType.DMA((4, PLANES, 4)),
            pltpu.SemaphoreType.DMA((2, GROUP)),
            pltpu.SemaphoreType.DMA((2,)),
        ],
        compiler_params=pltpu.CompilerParams(
            collective_id=0, has_side_effects=True, vmem_limit_bytes=56 * 1024 * 1024
        ),
        cost_estimate=pl.CostEstimate(
            flops=2 * rows * width * (q_cols + 2 * kv_cols) + 4 * rows * rows * GROUP * q_cols,
            bytes_accessed=2 * width * (q_cols + 2 * kv_cols),
            transcendentals=rows * rows * GROUP * heads,
        ),
    )(owned_block, hidden, norm_gain, query_weight, key_weight, value_weight, jnp.asarray(rope_table(rows)))


def solution(mesh):
    return jax.shard_map(
        section,
        mesh=mesh,
        in_specs=(
            P("seq", None),
            P("segment", None),
            P("segment", None, None),
            P("segment", None, None),
            P("segment", None, None),
            P(),
        ),
        out_specs=P("segment", "seq", None),
        check_vma=False,
    )
```
